128 devices in a mesh: head: 4 (over y), ctx: 32 (over x, z, core).
Axes of the slice: x: 4, y: 4, z: 4, core: 2. Of those that a mesh axis runs over, the one named last changes fastest.
Arguments:
- queries: bfloat16 [65536, 8192], P('ctx', 'head'), may hold values from -80 to 80
- keys_cache: bfloat16 [65536, 1024], P('ctx', 'head'), may hold values from -6 to 6
- values_cache: bfloat16 [65536, 1024], P('ctx', 'head'), may hold values from -6 to 6
- doc_ids: int32 [65536], replicated, may hold values from 0 to 3, as said below
- query_owner: int32 [2], replicated, may hold values from 0 to 31
- query_offset: int32 [2], replicated, may hold values from 0 to 1536
- out_weight: bfloat16 [8192, 8192], P('head', 'ctx'), may hold values from -0.25 to 0.25
Outputs:
- projected: bfloat16 [1024, 8192], P('head', 'ctx')
The draws below stay inside these ranges and needn't reach their ends.
Inputs may be any that keep to these rules, and one draw needn't show every extreme that they name: `doc_ids`: document numbers never fall along the sequence and start at 0; the last document begins before position 1984.
All inputs are finite; a program needn't handle non-finite values.
Results may differ from the reference program's by a relative error of at most 0.0051.
Values may be sent and summed in bfloat16 or wider, within the bound.
A program may use at most 576 MiB of HBM per device.

```python
import math
import jax
import jax.numpy as jnp
from jax import lax

D = 8192
HQ = 64
KVH = 8
DH = 128
QC = 512
NCH = 2
DOCS = 4
S_DEV = 2048
TOKENS = 65536
N_CTX = 32


def draw_doc_ids(key, part):
    key = jax.random.fold_in(key, 7)
    bounds = jax.random.randint(key, (DOCS - 1,), 1, S_DEV - 64)
    positions = jnp.arange(TOKENS, dtype=jnp.int32)
    return jnp.sum((positions[:, None] >= bounds[None, :]).astype(jnp.int32), axis=1).astype(jnp.int32)


def draw_query_owner(key, part):
    key = jax.random.fold_in(key, 19)
    which_key = jax.random.fold_in(key, 1)
    other_key = jax.random.fold_in(key, 2)
    others = jax.random.randint(other_key, (NCH,), 0, N_CTX)
    last_block = jax.random.randint(which_key, (), 0, NCH)
    blocks = jnp.arange(NCH, dtype=jnp.int32)
    return jnp.where(blocks == last_block, N_CTX - 1, others).astype(jnp.int32)


def draw_queries(key, part):
    first_key = jax.random.fold_in(key, 1)
    shape = (TOKENS, HQ * DH)
    return jnp.clip(jax.random.normal(first_key, shape, jnp.float32) * 2.5, -15.0, 15.0).astype(jnp.bfloat16)


def draw_keys_cache(key, part):
    first_key = jax.random.fold_in(key, 3)
    shape = (TOKENS, KVH * DH)
    return jnp.clip(jax.random.normal(first_key, shape, jnp.float32), -6.0, 6.0).astype(jnp.bfloat16)


def level_of(rng, extent, cuts, low, high):
    gain, own = 1.0, jax.random.fold_in(rng, 6)
    for dim, parts in cuts:
        draws = jnp.exp(jax.random.uniform(jax.random.fold_in(own, dim), (parts,), jnp.float32, low / len(cuts), high / len(cuts)))
        gain = gain * jnp.repeat(draws, extent[dim] // parts).reshape([-1 if axis == dim else 1 for axis in range(len(extent))])
    return gain


def noise(stream_key, shape, deviation, most, shards=(), kind=jnp.bfloat16):
    gain = level_of(stream_key, shape, shards, -0.22, 0.18) if shards else 1.0
    values = jax.random.normal(stream_key, shape, jnp.float32) * deviation * gain
    return jnp.minimum(jnp.maximum(values, -most), most).astype(kind)


def setup_inputs(seed: int = 0) -> dict:
    seeds = jax.random.split(jax.random.key(seed), 8)
    queries = draw_queries(jax.random.fold_in(seeds[7], 71), 0)
    keys_cache = draw_keys_cache(jax.random.fold_in(seeds[7], 71), 0)
    values_cache = noise(seeds[2], (TOKENS, KVH * DH), 1.0, 6.0, ((0, 32), (1, 4)))
    doc_ids = draw_doc_ids(jax.random.fold_in(seeds[7], 71), 0)
    query_owner = draw_query_owner(jax.random.fold_in(seeds[7], 71), 0)
    query_offset = jax.random.randint(seeds[5], (NCH,), 0, S_DEV - QC + 1).astype(jnp.int32)
    out_weight = noise(seeds[6], (HQ * DH, D), (HQ * DH // 16) ** -0.5, 0.25, ((0, 4), (1, 32)))
    return dict(queries=queries, keys_cache=keys_cache, values_cache=values_cache, doc_ids=doc_ids, query_owner=query_owner, query_offset=query_offset, out_weight=out_weight)


def reference(queries, keys_cache, values_cache, doc_ids, query_owner, query_offset, out_weight):
    group_size = HQ // KVH
    score_scale = 1.0 / math.sqrt(DH)
    results = []
    for which in range(NCH):
        start = (query_owner[which] * S_DEV + query_offset[which]).astype(jnp.int32)
        query_rows = lax.dynamic_slice_in_dim(queries, start, QC, 0)
        query_pos = start + jnp.arange(QC, dtype=jnp.int32)
        query_doc = lax.dynamic_slice_in_dim(doc_ids, start, QC, 0)
        query_heads = query_rows.astype(jnp.float32).reshape(QC, KVH, group_size, DH)

        def visit(carry, index):
            run_max, run_total, run_out = carry
            first = (index * S_DEV).astype(jnp.int32)
            key_block = lax.dynamic_slice_in_dim(keys_cache, first, S_DEV, 0).astype(jnp.float32).reshape(S_DEV, KVH, DH)
            value_block = lax.dynamic_slice_in_dim(values_cache, first, S_DEV, 0).astype(jnp.float32).reshape(S_DEV, KVH, DH)
            key_pos = first + jnp.arange(S_DEV, dtype=jnp.int32)
            key_doc = lax.dynamic_slice_in_dim(doc_ids, first, S_DEV, 0)
            allowed = (key_pos[None, :] <= query_pos[:, None]) & (key_doc[None, :] == query_doc[:, None])
            allowed = allowed[:, None, None, :]
            scores = jnp.einsum('qkgd,skd->qkgs', query_heads, key_block, precision=lax.Precision.HIGHEST) * score_scale
            masked = jnp.where(allowed, scores, jnp.float32(-1e+30))
            block_max = lax.optimization_barrier(jnp.max(masked, axis=-1))
            weights = jnp.where(allowed, jnp.exp(masked - block_max[..., None]), jnp.float32(0.0))
            block_total = lax.optimization_barrier(jnp.sum(weights, axis=-1))
            rounded = weights.astype(jnp.bfloat16).astype(jnp.float32)
            block_out = jnp.einsum('qkgs,skd->qkgd', rounded, value_block, precision=lax.Precision.HIGHEST)
            new_max = jnp.maximum(run_max, block_max)
            old_factor = jnp.exp(run_max - new_max)
            new_factor = jnp.exp(block_max - new_max)
            run_total = run_total * old_factor + block_total * new_factor
            run_out = run_out * old_factor[..., None] + block_out * new_factor[..., None]
            return ((new_max, run_total, run_out), None)
        init = (jnp.full((QC, KVH, group_size), -1e+30, jnp.float32), jnp.zeros((QC, KVH, group_size), jnp.float32), jnp.zeros((QC, KVH, group_size, DH), jnp.float32))
        (row_max, row_total, row_out), unused = lax.scan(visit, init, jnp.arange(N_CTX, dtype=jnp.int32))
        attention = (row_out / row_total[..., None]).reshape(QC, HQ * DH).astype(jnp.bfloat16)
        results.append(attention)
    attention = jnp.concatenate(results, axis=0)
    return jnp.dot(attention, out_weight, preferred_element_type=jnp.float32).astype(jnp.bfloat16)
```

```python
import functools
import math

import jax
import jax.numpy as jnp
from jax import lax
from jax.experimental import pallas as pl
from jax.experimental.pallas import tpu as pltpu
from jax.sharding import PartitionSpec as P

DH = 128
QC = 512
NCH = 2
R = 128
NC = NCH * QC // R
G = 8
MT = 512
HIDE = -1e30
SCALE = math.log2(math.e) / math.sqrt(DH)
MESH = pl.DeviceIdType.MESH
LEAD = 6
TRAIL = 6

S0, S1, S2, G1, G2, G3, O0, O1, O2, H1, H2, H3, Y = range(13)


def kernel(
    q_own, k_ref, v_ref, w_ref, lo_ref, hi_ref, out_ref,
    kx, vx, qx, s_buf, p_buf,
    u_buf, r1, t_buf, r2, q_full,
    o_send, o_recv, o_own, o_mix, o_two, w_col, o1_send, r1o, o2_send, r2o, a_full,
    y_send, y_recv, send, recv,
):
    shard = k_ref.shape[0]
    me = lax.axis_index("ctx")
    hd = lax.axis_index("head")
    core = lax.rem(me, 2)
    z = lax.rem(me // 2, 4)
    x = me // 8
    mine, theirs = core * G, (1 - core) * G

    def at_x(d):
        return {"ctx": (lax.rem(x + d, 4) * 4 + z) * 2 + core}

    def at_z(d):
        return {"ctx": (x * 4 + lax.rem(z + d, 4)) * 2 + core}

    partner = {"ctx": me + 1 - 2 * core}

    def at_y(d):
        return {"head": lax.rem(hd + d, 4)}

    barrier = pltpu.get_barrier_semaphore()
    for d in (1, 2, 3):
        for dev in (at_x(d), at_z(d), at_y(d)):
            pl.semaphore_signal(barrier, inc=1, device_id=dev, device_id_type=MESH)
    pl.semaphore_signal(barrier, inc=1, device_id=partner, device_id_type=MESH)

    eye = lax.broadcasted_iota(jnp.int32, (R, R), 0) == lax.broadcasted_iota(jnp.int32, (R, R), 1)
    for j in range(2):
        kx[j, 0:DH, :] = k_ref[:, j * DH : (j + 1) * DH].T
        vx[j, :, 0:DH] = v_ref[:, j * DH : (j + 1) * DH]
        vx[j, :, DH : 2 * DH] = jnp.ones((shard, DH), jnp.bfloat16)
    for g in range(G):
        qx[g * R : (g + 1) * R, DH : 2 * DH] = jnp.where(eye, 1.0, 0.0).astype(jnp.bfloat16)

    pl.semaphore_wait(barrier, 10)

    def put(src, dst, step, c, dev):
        pltpu.make_async_remote_copy(
            src_ref=src, dst_ref=dst, send_sem=send.at[step, c], recv_sem=recv.at[step, c],
            device_id=dev, device_id_type=MESH,
        ).start()

    def get(like, step, c):
        pltpu.make_async_copy(like, like, send.at[step, c]).wait()
        pltpu.make_async_copy(like, like, recv.at[step, c]).wait()

    def rows(c):
        return pl.ds(pl.multiple_of(c * R, R), R)

    def quarter(i):
        return pl.ds(pl.multiple_of(i * 32, 32), 32)

    def q0_start(c):
        put(q_own.at[pl.ds(theirs, G), rows(c)], u_buf.at[c], S0, c, partner)

    def q1_start(c):
        get(u_buf.at[c], S0, c)
        for g in range(G):
            u_buf[c, g] = u_buf[c, g] + q_own[mine + g, rows(c), :]
        for d in (1, 2, 3):
            put(u_buf.at[c, lax.rem(x + d, 4)], r1.at[c, d - 1], S1, c, at_x(d))
            put(u_buf.at[c, 4 + lax.rem(z + d, 4)], r1.at[c, 2 + d], S1, c, at_z(d))

    def q2_start(c):
        get(r1.at[c], S1, c)
        t_buf[c, 0] = (u_buf[c, x] + r1[c, 0]) + (r1[c, 1] + r1[c, 2])
        t_buf[c, 1] = (u_buf[c, 4 + z] + r1[c, 3]) + (r1[c, 4] + r1[c, 5])
        for d in (1, 2, 3):
            put(t_buf.at[c, 0, quarter(lax.rem(z + d, 4))], r2.at[c, d - 1], S2, c, at_z(d))
            put(t_buf.at[c, 1, quarter(lax.rem(x + d, 4))], r2.at[c, 2 + d], S2, c, at_x(d))

    def gather1(full, c, step):
        a = full.at[c, mine + x, quarter(z)]
        b = full.at[c, mine + 4 + z, quarter(x)]
        for d in (1, 2, 3):
            put(a, a, step, c, at_z(d))
            put(b, b, step, c, at_x(d))

    def gather2(full, c, step):
        get(r2.at[c], step - 1, c)
        a, b = full.at[c, mine + x], full.at[c, mine + 4 + z]
        for d in (1, 2, 3):
            put(a, a, step, c, at_x(d))
            put(b, b, step, c, at_z(d))

    def gather3(full, c, step):
        get(r1.at[c], step - 1, c)
        half = full.at[c, pl.ds(mine, G)]
        put(half, half, step, c, partner)

    def q3_start(c):
        get(r2.at[c], S2, c)
        q_full[c, mine + x, quarter(z), :] = (t_buf[c, 0, quarter(z), :] + r2[c, 0]) + (r2[c, 1] + r2[c, 2])
        q_full[c, mine + 4 + z, quarter(x), :] = (t_buf[c, 1, quarter(x), :] + r2[c, 3]) + (r2[c, 4] + r2[c, 5])
        gather1(q_full, c, G1)

    def hide(c):
        lo = jnp.broadcast_to(lo_ref[pl.ds(c, 1), :], (R, R)).T
        hi = jnp.broadcast_to(hi_ref[pl.ds(c, 1), :], (R, R)).T
        lane = lax.broadcasted_iota(jnp.int32, (R, R), 1).astype(jnp.float32)
        for i in range(shard // R):
            pos = lane + float(i * R)
            bias = jnp.where((pos >= lo) & (pos <= hi), 0.0, HIDE).astype(jnp.bfloat16)
            for j in range(2):
                kx[j, DH : 2 * DH, i * R : (i + 1) * R] = bias

    def attend(c, j, dest):
        first = j * G
        for g in range(G):
            qx[g * R : (g + 1) * R, 0:DH] = q_full[c, first + g]
        tiles = G * R // MT

        def score(t):
            s_buf[t] = jnp.dot(qx[t * MT : (t + 1) * MT, :], kx[j], preferred_element_type=jnp.float32)

        score(0)
        for t in range(tiles):
            if t + 1 < tiles:
                score(t + 1)
            s = s_buf[t]
            top = jnp.max(s, axis=1, keepdims=True) * SCALE
            p_buf[t] = jnp.exp2(s * SCALE - top).astype(jnp.bfloat16)
            o = jnp.dot(p_buf[t], vx[j], preferred_element_type=jnp.float32)
            total = o[:, DH : 2 * DH]
            mean = o[:, 0:DH] / total
            lse = top + jnp.log2(total)
            for i in range(MT // R):
                g = t * (MT // R) + i
                dest[g, 0:R, :] = mean[i * R : (i + 1) * R]
                flat = jnp.sum(jnp.where(eye, lse[i * R : (i + 1) * R], 0.0), axis=0, keepdims=True)
                dest[g, R : R + 8, :] = jnp.broadcast_to(flat, (8, R))

    def column(v):
        return jnp.broadcast_to(v, (R, R)).T

    def merge_stats(parts):
        top = functools.reduce(jnp.maximum, parts)
        ws = [jnp.exp2(p - top) for p in parts]
        total = functools.reduce(jnp.add, ws)
        return [w / total for w in ws], top + jnp.log2(total)

    def pieces3(v):
        a = v.astype(jnp.bfloat16)
        rest = v - a.astype(jnp.float32)
        b = rest.astype(jnp.bfloat16)
        c = (rest - b.astype(jnp.float32)).astype(jnp.bfloat16)
        row = lax.broadcasted_iota(jnp.int32, (16, R), 0)
        full = [jnp.broadcast_to(p.astype(jnp.float32), (16, R)) for p in (a, b, c)]
        return jnp.where(row == 0, full[0], jnp.where(row == 1, full[1], jnp.where(row == 2, full[2], 0.0))).astype(jnp.bfloat16)

    def whole3(block):
        f = block.astype(jnp.float32)
        return (f[0:1] + f[1:2]) + f[2:3]

    def o1_start(c):
        get(o_recv.at[c], O0, c)
        for g in range(G):
            (wa, wb), lse = merge_stats([o_own[g, R : R + 1, :], o_recv[c, g, R : R + 1, :]])
            mixed = o_own[g, 0:R, :] * column(wa) + o_recv[c, g, 0:R, :] * column(wb)
            o_mix[g, 0:R, :] = mixed
            o_mix[g, R : R + 8, :] = jnp.broadcast_to(lse, (8, R))
            o1_send[c, g, 0:R, :] = mixed.astype(jnp.bfloat16)
            o1_send[c, g, R : R + 16, :] = pieces3(lse)
        for d in (1, 2, 3):
            put(o1_send.at[c, lax.rem(x + d, 4)], r1o.at[c, d - 1], O1, c, at_x(d))
            put(o1_send.at[c, 4 + lax.rem(z + d, 4)], r1o.at[c, 2 + d], O1, c, at_z(d))

    def o2_start(c):
        get(r1o.at[c], O1, c)
        for i, at in ((0, x), (1, 4 + z)):
            stats = [o_mix[at, R : R + 1, :]] + [whole3(r1o[c, 3 * i + d, R : R + 16, :]) for d in range(3)]
            ws, lse = merge_stats(stats)
            mixed = o_mix[at, 0:R, :] * column(ws[0])
            for d in range(3):
                mixed += r1o[c, 3 * i + d, 0:R, :].astype(jnp.float32) * column(ws[1 + d])
            o_two[i, 0:R, :] = mixed
            o_two[i, R : R + 8, :] = jnp.broadcast_to(lse, (8, R))
            coded = pieces3(lse)
            for q in range(4):
                o2_send[c, i, q, 0:32, :] = mixed[q * 32 : (q + 1) * 32].astype(jnp.bfloat16)
                o2_send[c, i, q, 32:48, :] = coded
        for d in (1, 2, 3):
            zd, xd = lax.rem(z + d, 4), lax.rem(x + d, 4)
            put(o2_send.at[c, 0, zd], r2o.at[c, d - 1], O2, c, at_z(d))
            put(o2_send.at[c, 1, xd], r2o.at[c, 2 + d], O2, c, at_x(d))

    def o3_start(c):
        get(r2o.at[c], O2, c)
        for i, at, part in ((0, x, z), (1, 4 + z, x)):
            stats = [o_two[i, R : R + 1, :]] + [whole3(r2o[c, 3 * i + d, 32:48, :]) for d in range(3)]
            ws, _ = merge_stats(stats)
            for d in range(4):
                w_col[d] = column(ws[d])
            mixed = o_two[i, quarter(part), :] * w_col[0, quarter(part), :]
            for d in range(3):
                mixed += r2o[c, 3 * i + d, 0:32, :].astype(jnp.float32) * w_col[1 + d, quarter(part), :]
            a_full[c, mine + at, quarter(part), :] = mixed.astype(jnp.bfloat16)
        gather1(a_full, c, H1)

    def project(c):
        get(a_full.at[c, pl.ds(0, G)], H3, c)
        acc = jnp.zeros((R, w_ref.shape[1]), jnp.float32)
        for h in range(2 * G):
            acc += jnp.dot(a_full[c, h], w_ref[h * DH : (h + 1) * DH, :], preferred_element_type=jnp.float32)
        y_send[c] = acc
        owner = c // 2
        slot = lax.rem(c, 2)
        d = lax.rem(owner - hd + 4, 4)

        @pl.when(d > 0)
        def _():
            put(y_send.at[c], y_recv.at[d - 1, slot], Y, c, at_y(d))

    def slot(t, carry):
        def when(c, do):
            pl.when((c >= 0) & (c < NC))(functools.partial(do, c))

        when(t, lambda c: get(u_buf.at[c], G3, c))
        when(t + 1, lambda c: gather3(q_full, c, G3))
        when(t + 2, lambda c: gather2(q_full, c, G2))
        when(t + 3, q3_start)
        when(t + 4, q2_start)
        when(t + 5, q1_start)
        when(t + 6, q0_start)

        def first(c):
            hide(c)
            attend(c, 1 - core, o_send)
            put(o_send, o_recv.at[c], O0, c, partner)

        when(t, first)
        when(t, lambda c: attend(c, core, o_own))
        when(t - 5, project)
        when(t - 4, lambda c: gather3(a_full, c, H3))
        when(t - 3, lambda c: gather2(a_full, c, H2))
        when(t - 2, o3_start)
        when(t - 1, o2_start)
        when(t, o1_start)
        return carry

    lax.fori_loop(-LEAD, NC + TRAIL - 1, slot, 0)

    for c in range(NC):
        d = lax.rem(c // 2 - hd + 4, 4)

        @pl.when(d > 0)
        def _():
            pltpu.make_async_copy(y_send.at[c], y_send.at[c], send.at[Y, c]).wait()

    for i in range(2):
        c = hd * 2 + i
        pltpu.make_async_copy(y_recv.at[:, i], y_recv.at[:, i], recv.at[Y, c]).wait()
        total = (y_send[c] + y_recv[0, i]) + (y_recv[1, i] + y_recv[2, i])
        out_ref[i * R : (i + 1) * R, :] = total.astype(jnp.bfloat16)


def per_device(queries, keys_cache, values_cache, doc_ids, query_owner, query_offset, out_weight):
    me = lax.axis_index("ctx")
    shard = keys_cache.shape[0]
    starts = query_owner * shard + query_offset
    own, positions, docs = [], [], []
    for which in range(NCH):
        block = lax.dynamic_slice_in_dim(queries, query_offset[which], QC, 0)
        own.append(jnp.where(query_owner[which] == me, block, jnp.zeros_like(block)))
        positions.append(starts[which] + jnp.arange(QC, dtype=jnp.int32))
        docs.append(lax.dynamic_slice_in_dim(doc_ids, starts[which], QC, 0))
    q_own = jnp.concatenate(own, 0).reshape(NC * R, 2 * G, DH).transpose(1, 0, 2)
    position, doc = jnp.concatenate(positions), jnp.concatenate(docs)
    early = doc_ids[:shard]
    begin = jnp.zeros_like(position)
    for d in range(1, 4):
        begin = jnp.where(doc == d, jnp.sum((early < d).astype(jnp.int32)), begin)
    lo = (begin - me * shard).astype(jnp.float32).reshape(NC, R)
    hi = (position - me * shard).astype(jnp.float32).reshape(NC, R)

    width = out_weight.shape[1]
    bf, f32 = jnp.bfloat16, jnp.float32
    scratch = [
        pltpu.VMEM((2, 2 * DH, shard), bf),
        pltpu.VMEM((2, shard, 2 * DH), bf),
        pltpu.VMEM((G * R, 2 * DH), bf),
        pltpu.VMEM((2, MT, shard), f32),
        pltpu.VMEM((2, MT, shard), bf),
        pltpu.VMEM((NC, G, R, DH), bf),
        pltpu.VMEM((NC, 6, R, DH), bf),
        pltpu.VMEM((NC, 2, R, DH), bf),
        pltpu.VMEM((NC, 6, 32, DH), bf),
        pltpu.VMEM((NC, 2 * G, R, DH), bf),
        pltpu.VMEM((G, R + 8, DH), f32),
        pltpu.VMEM((NC, G, R + 8, DH), f32),
        pltpu.VMEM((G, R + 8, DH), f32),
        pltpu.VMEM((G, R + 8, DH), f32),
        pltpu.VMEM((2, R + 8, DH), f32),
        pltpu.VMEM((4, R, DH), f32),
        pltpu.VMEM((NC, G, R + 16, DH), bf),
        pltpu.VMEM((NC, 6, R + 16, DH), bf),
        pltpu.VMEM((NC, 2, 4, 48, DH), bf),
        pltpu.VMEM((NC, 6, 48, DH), bf),
        pltpu.VMEM((NC, 2 * G, R, DH), bf),
        pltpu.VMEM((NC, R, width), f32),
        pltpu.VMEM((3, 2, R, width), f32),
        pltpu.SemaphoreType.DMA((13, NC)),
        pltpu.SemaphoreType.DMA((13, NC)),
    ]
    vmem = pl.BlockSpec(memory_space=pltpu.VMEM)
    return pl.pallas_call(
        kernel,
        out_shape=jax.ShapeDtypeStruct((NC * R // 4, width), bf),
        in_specs=[vmem] * 6,
        out_specs=vmem,
        scratch_shapes=scratch,
        compiler_params=pltpu.CompilerParams(
            collective_id=0, has_side_effects=True, vmem_limit_bytes=60 * 2**20
        ),
    )(q_own, keys_cache, values_cache, out_weight, lo, hi)


def solution(mesh):
    placed = (P("ctx", "head"), P("ctx", "head"), P("ctx", "head"), P(), P(), P(), P("head", "ctx"))
    return jax.shard_map(
        per_device, mesh=mesh, in_specs=placed, out_specs=P("head", "ctx"), check_vma=False
    )
```

```python
import functools
import math

import jax
import jax.numpy as jnp
from jax import lax
from jax.experimental import pallas as pl
from jax.experimental.pallas import tpu as pltpu
from jax.sharding import PartitionSpec as P

DH = 128
QC = 512
NCH = 2
R = 128
NC = NCH * QC // R
G = 8
MT = 512
HIDE = -1e30
SCALE = math.log2(math.e) / math.sqrt(DH)
MESH = pl.DeviceIdType.MESH
LEAD = 6
TRAIL = 6

S0, S1, S2, G1, G2, G3, O0, O1, O2, H1, H2, H3, Y = range(13)


def kernel(
    queries, keys, values, weight, early_ref, owner_ref, offset_ref, out_ref,
    q_all, k_ref, v_ref, w_ref, load, q_send, q_mine,
    kx, vx, qx, s_buf, p_buf,
    u_buf, r1, t_buf, r2, q_full,
    o_send, o_recv, o_own, o_mix, o_two, w_col, o1_send, r1o, o2_send, r2o, a_full,
    y_send, y_recv, send, recv,
):
    shard = k_ref.shape[0]
    loads = [
        pltpu.make_async_copy(queries, q_all, load.at[0]),
        pltpu.make_async_copy(keys, k_ref, load.at[1]),
        pltpu.make_async_copy(values, v_ref, load.at[2]),
        pltpu.make_async_copy(weight, w_ref, load.at[3]),
    ]
    for one in loads:
        one.start()
    me = lax.axis_index("ctx")
    hd = lax.axis_index("head")
    core = lax.rem(me, 2)
    z = lax.rem(me // 2, 4)
    x = me // 8
    mine, theirs = core * G, (1 - core) * G

    def at_x(d):
        return {"ctx": (lax.rem(x + d, 4) * 4 + z) * 2 + core}

    def at_z(d):
        return {"ctx": (x * 4 + lax.rem(z + d, 4)) * 2 + core}

    partner = {"ctx": me + 1 - 2 * core}

    def at_y(d):
        return {"head": lax.rem(hd + d, 4)}

    barrier = pltpu.get_barrier_semaphore()
    for d in (1, 2, 3):
        for dev in (at_x(d), at_z(d), at_y(d)):
            pl.semaphore_signal(barrier, inc=1, device_id=dev, device_id_type=MESH)
    pl.semaphore_signal(barrier, inc=1, device_id=partner, device_id_type=MESH)

    eye = lax.broadcasted_iota(jnp.int32, (R, R), 0) == lax.broadcasted_iota(jnp.int32, (R, R), 1)

    def prepare():
        for one in loads[1:]:
            one.wait()
        for j in range(2):
            kx[j, 0:DH, :] = k_ref[:, j * DH : (j + 1) * DH].T
            vx[j, :, 0:DH] = v_ref[:, j * DH : (j + 1) * DH]
            vx[j, :, DH : 2 * DH] = jnp.ones((shard, DH), jnp.bfloat16)
        for g in range(G):
            qx[g * R : (g + 1) * R, DH : 2 * DH] = jnp.where(eye, 1.0, 0.0).astype(jnp.bfloat16)

    loads[0].wait()
    pl.semaphore_wait(barrier, 10)

    def put(src, dst, step, c, dev):
        pltpu.make_async_remote_copy(
            src_ref=src, dst_ref=dst, send_sem=send.at[step, c], recv_sem=recv.at[step, c],
            device_id=dev, device_id_type=MESH,
        ).start()

    def get(like, step, c):
        pltpu.make_async_copy(like, like, send.at[step, c]).wait()
        pltpu.make_async_copy(like, like, recv.at[step, c]).wait()

    def quarter(i):
        return pl.ds(pl.multiple_of(i * 32, 32), 32)

    def q0_start(c):
        which = c // (NC // NCH)
        row = lax.broadcasted_iota(jnp.int32, (R, shard), 0) + (offset_ref[which] + lax.rem(c, NC // NCH) * R)
        here = (jnp.zeros((R, shard), jnp.int32) + owner_ref[which]) == me
        hit = (row == lax.broadcasted_iota(jnp.int32, (R, shard), 1)) & here
        pick = jnp.where(hit, 1.0, 0.0).astype(jnp.bfloat16)
        got = jnp.dot(pick, q_all[...], preferred_element_type=jnp.float32).astype(jnp.bfloat16)
        for g in range(G):
            low, high = got[:, g * DH : (g + 1) * DH], got[:, (G + g) * DH : (G + g + 1) * DH]
            q_mine[g] = jnp.where(core == 0, low, high)
            q_send[g] = jnp.where(core == 0, high, low)
        put(q_send, u_buf.at[c], S0, c, partner)

    def q1_start(c):
        get(u_buf.at[c], S0, c)
        for g in range(G):
            u_buf[c, g] = u_buf[c, g] + q_mine[g]
        for d in (1, 2, 3):
            put(u_buf.at[c, lax.rem(x + d, 4)], r1.at[c, d - 1], S1, c, at_x(d))
            put(u_buf.at[c, 4 + lax.rem(z + d, 4)], r1.at[c, 2 + d], S1, c, at_z(d))

    def q2_start(c):
        get(r1.at[c], S1, c)
        t_buf[c, 0] = (u_buf[c, x] + r1[c, 0]) + (r1[c, 1] + r1[c, 2])
        t_buf[c, 1] = (u_buf[c, 4 + z] + r1[c, 3]) + (r1[c, 4] + r1[c, 5])
        for d in (1, 2, 3):
            put(t_buf.at[c, 0, quarter(lax.rem(z + d, 4))], r2.at[c, d - 1], S2, c, at_z(d))
            put(t_buf.at[c, 1, quarter(lax.rem(x + d, 4))], r2.at[c, 2 + d], S2, c, at_x(d))

    def gather1(full, c, step):
        a = full.at[c, mine + x, quarter(z)]
        b = full.at[c, mine + 4 + z, quarter(x)]
        for d in (1, 2, 3):
            put(a, a, step, c, at_z(d))
            put(b, b, step, c, at_x(d))

    def gather2(full, c, step):
        get(r2.at[c], step - 1, c)
        a, b = full.at[c, mine + x], full.at[c, mine + 4 + z]
        for d in (1, 2, 3):
            put(a, a, step, c, at_x(d))
            put(b, b, step, c, at_z(d))

    def gather3(full, c, step):
        get(r1.at[c], step - 1, c)
        half = full.at[c, pl.ds(mine, G)]
        put(half, half, step, c, partner)

    def q3_start(c):
        get(r2.at[c], S2, c)
        q_full[c, mine + x, quarter(z), :] = (t_buf[c, 0, quarter(z), :] + r2[c, 0]) + (r2[c, 1] + r2[c, 2])
        q_full[c, mine + 4 + z, quarter(x), :] = (t_buf[c, 1, quarter(x), :] + r2[c, 3]) + (r2[c, 4] + r2[c, 5])
        gather1(q_full, c, G1)

    def hide(c):
        which = c // (NC // NCH)
        begin = owner_ref[which] * shard + offset_ref[which] + lax.rem(c, NC // NCH) * R
        pos = (lax.broadcasted_iota(jnp.int32, (R, R), 0) + begin).astype(jnp.float32)
        lo = jnp.zeros((R, R), jnp.float32)
        early = early_ref[...]
        for d in range(1, 4):
            bound = jnp.sum(jnp.where(early < d, 1.0, 0.0), axis=0, keepdims=True)
            bound = jnp.broadcast_to(jnp.sum(bound, axis=1, keepdims=True), (R, R))
            lo = jnp.where((bound <= pos) & (bound < float(shard)), jnp.maximum(lo, bound), lo)
        here = (jnp.zeros((R, R), jnp.int32) + me * shard).astype(jnp.float32)
        lo, hi = lo - here, pos - here
        lane = lax.broadcasted_iota(jnp.int32, (R, R), 1).astype(jnp.float32)
        for i in range(shard // R):
            pos = lane + float(i * R)
            bias = jnp.where((pos >= lo) & (pos <= hi), 0.0, HIDE).astype(jnp.bfloat16)
            for j in range(2):
                kx[j, DH : 2 * DH, i * R : (i + 1) * R] = bias

    def attend(c, j, dest):
        first = j * G
        for g in range(G):
            qx[g * R : (g + 1) * R, 0:DH] = q_full[c, first + g]
        tiles = G * R // MT

        def score(t):
            s_buf[t] = jnp.dot(qx[t * MT : (t + 1) * MT, :], kx[j], preferred_element_type=jnp.float32)

        score(0)
        for t in range(tiles):
            if t + 1 < tiles:
                score(t + 1)
            s = s_buf[t]
            top = jnp.max(s, axis=1, keepdims=True) * SCALE
            p_buf[t] = jnp.exp2(s * SCALE - top).astype(jnp.bfloat16)
            o = jnp.dot(p_buf[t], vx[j], preferred_element_type=jnp.float32)
            total = o[:, DH : 2 * DH]
            mean = o[:, 0:DH] / total
            lse = top + jnp.log2(total)
            for i in range(MT // R):
                g = t * (MT // R) + i
                dest[g, 0:R, :] = mean[i * R : (i + 1) * R]
                flat = jnp.sum(jnp.where(eye, lse[i * R : (i + 1) * R], 0.0), axis=0, keepdims=True)
                dest[g, R : R + 8, :] = jnp.broadcast_to(flat, (8, R))

    def column(v):
        return jnp.broadcast_to(v, (R, R)).T

    def merge_stats(parts):
        top = functools.reduce(jnp.maximum, parts)
        ws = [jnp.exp2(p - top) for p in parts]
        total = functools.reduce(jnp.add, ws)
        return [w / total for w in ws], top + jnp.log2(total)

    def pieces3(v):
        a = v.astype(jnp.bfloat16)
        rest = v - a.astype(jnp.float32)
        b = rest.astype(jnp.bfloat16)
        c = (rest - b.astype(jnp.float32)).astype(jnp.bfloat16)
        row = lax.broadcasted_iota(jnp.int32, (16, R), 0)
        full = [jnp.broadcast_to(p.astype(jnp.float32), (16, R)) for p in (a, b, c)]
        return jnp.where(row == 0, full[0], jnp.where(row == 1, full[1], jnp.where(row == 2, full[2], 0.0))).astype(jnp.bfloat16)

    def whole3(block):
        f = block.astype(jnp.float32)
        return (f[0:1] + f[1:2]) + f[2:3]

    def o1_start(c):
        get(o_recv.at[c], O0, c)
        for g in range(G):
            (wa, wb), lse = merge_stats([o_own[g, R : R + 1, :], o_recv[c, g, R : R + 1, :]])
            mixed = o_own[g, 0:R, :] * column(wa) + o_recv[c, g, 0:R, :] * column(wb)
            o_mix[g, 0:R, :] = mixed
            o_mix[g, R : R + 8, :] = jnp.broadcast_to(lse, (8, R))
            o1_send[c, g, 0:R, :] = mixed.astype(jnp.bfloat16)
            o1_send[c, g, R : R + 16, :] = pieces3(lse)
        for d in (1, 2, 3):
            put(o1_send.at[c, lax.rem(x + d, 4)], r1o.at[c, d - 1], O1, c, at_x(d))
            put(o1_send.at[c, 4 + lax.rem(z + d, 4)], r1o.at[c, 2 + d], O1, c, at_z(d))

    def o2_start(c):
        get(r1o.at[c], O1, c)
        for i, at in ((0, x), (1, 4 + z)):
            stats = [o_mix[at, R : R + 1, :]] + [whole3(r1o[c, 3 * i + d, R : R + 16, :]) for d in range(3)]
            ws, lse = merge_stats(stats)
            mixed = o_mix[at, 0:R, :] * column(ws[0])
            for d in range(3):
                mixed += r1o[c, 3 * i + d, 0:R, :].astype(jnp.float32) * column(ws[1 + d])
            o_two[i, 0:R, :] = mixed
            o_two[i, R : R + 8, :] = jnp.broadcast_to(lse, (8, R))
            coded = pieces3(lse)
            for q in range(4):
                o2_send[c, i, q, 0:32, :] = mixed[q * 32 : (q + 1) * 32].astype(jnp.bfloat16)
                o2_send[c, i, q, 32:48, :] = coded
        for d in (1, 2, 3):
            zd, xd = lax.rem(z + d, 4), lax.rem(x + d, 4)
            put(o2_send.at[c, 0, zd], r2o.at[c, d - 1], O2, c, at_z(d))
            put(o2_send.at[c, 1, xd], r2o.at[c, 2 + d], O2, c, at_x(d))

    def o3_start(c):
        get(r2o.at[c], O2, c)
        for i, at, part in ((0, x, z), (1, 4 + z, x)):
            stats = [o_two[i, R : R + 1, :]] + [whole3(r2o[c, 3 * i + d, 32:48, :]) for d in range(3)]
            ws, _ = merge_stats(stats)
            for d in range(4):
                w_col[d] = column(ws[d])
            mixed = o_two[i, quarter(part), :] * w_col[0, quarter(part), :]
            for d in range(3):
                mixed += r2o[c, 3 * i + d, 0:32, :].astype(jnp.float32) * w_col[1 + d, quarter(part), :]
            a_full[c, mine + at, quarter(part), :] = mixed.astype(jnp.bfloat16)
        gather1(a_full, c, H1)

    def project(c):
        get(a_full.at[c, pl.ds(0, G)], H3, c)
        acc = jnp.zeros((R, w_ref.shape[1]), jnp.float32)
        for h in range(2 * G):
            acc += jnp.dot(a_full[c, h], w_ref[h * DH : (h + 1) * DH, :], preferred_element_type=jnp.float32)
        y_send[c] = acc
        owner = c // 2
        slot = lax.rem(c, 2)
        d = lax.rem(owner - hd + 4, 4)

        @pl.when(d > 0)
        def _():
            put(y_send.at[c], y_recv.at[d - 1, slot], Y, c, at_y(d))

    def slot(t, carry):
        def when(c, do):
            pl.when((c >= 0) & (c < NC))(functools.partial(do, c))

        def first(c):
            get(u_buf.at[c], G3, c)
            hide(c)
            attend(c, 1 - core, o_send)
            put(o_send, o_recv.at[c], O0, c, partner)

        when(t, first)
        when(t + 1, lambda c: gather3(q_full, c, G3))
        when(t + 2, lambda c: gather2(q_full, c, G2))
        when(t + 3, q3_start)
        when(t + 4, q2_start)
        when(t + 5, q1_start)
        when(t + 6, q0_start)
        pl.when(t == 1 - LEAD)(prepare)
        when(t, lambda c: attend(c, core, o_own))
        when(t - 5, project)
        when(t - 4, lambda c: gather3(a_full, c, H3))
        when(t - 3, lambda c: gather2(a_full, c, H2))
        when(t - 2, o3_start)
        when(t - 1, o2_start)
        when(t, o1_start)
        return carry

    lax.fori_loop(-LEAD, NC + TRAIL - 1, slot, 0)

    for c in range(NC):
        d = lax.rem(c // 2 - hd + 4, 4)

        @pl.when(d > 0)
        def _():
            pltpu.make_async_copy(y_send.at[c], y_send.at[c], send.at[Y, c]).wait()

    for i in range(2):
        c = hd * 2 + i
        pltpu.make_async_copy(y_recv.at[:, i], y_recv.at[:, i], recv.at[Y, c]).wait()
        total = (y_send[c] + y_recv[0, i]) + (y_recv[1, i] + y_recv[2, i])
        out_ref[i * R : (i + 1) * R, :] = total.astype(jnp.bfloat16)


def per_device(queries, keys_cache, values_cache, doc_ids, query_owner, query_offset, out_weight):
    shard = keys_cache.shape[0]
    early = doc_ids[:shard].reshape(-1, DH)
    width = out_weight.shape[1]
    bf, f32 = jnp.bfloat16, jnp.float32
    scratch = [
        pltpu.VMEM(queries.shape, bf),
        pltpu.VMEM(keys_cache.shape, bf),
        pltpu.VMEM(values_cache.shape, bf),
        pltpu.VMEM(out_weight.shape, bf),
        pltpu.SemaphoreType.DMA((4,)),
        pltpu.VMEM((G, R, DH), bf),
        pltpu.VMEM((G, R, DH), bf),
        pltpu.VMEM((2, 2 * DH, shard), bf),
        pltpu.VMEM((2, shard, 2 * DH), bf),
        pltpu.VMEM((G * R, 2 * DH), bf),
        pltpu.VMEM((2, MT, shard), f32),
        pltpu.VMEM((2, MT, shard), bf),
        pltpu.VMEM((NC, G, R, DH), bf),
        pltpu.VMEM((NC, 6, R, DH), bf),
        pltpu.VMEM((NC, 2, R, DH), bf),
        pltpu.VMEM((NC, 6, 32, DH), bf),
        pltpu.VMEM((NC, 2 * G, R, DH), bf),
        pltpu.VMEM((G, R + 8, DH), f32),
        pltpu.VMEM((NC, G, R + 8, DH), f32),
        pltpu.VMEM((G, R + 8, DH), f32),
        pltpu.VMEM((G, R + 8, DH), f32),
        pltpu.VMEM((2, R + 8, DH), f32),
        pltpu.VMEM((4, R, DH), f32),
        pltpu.VMEM((NC, G, R + 16, DH), bf),
        pltpu.VMEM((NC, 6, R + 16, DH), bf),
        pltpu.VMEM((NC, 2, 4, 48, DH), bf),
        pltpu.VMEM((NC, 6, 48, DH), bf),
        pltpu.VMEM((NC, 2 * G, R, DH), bf),
        pltpu.VMEM((NC, R, width), f32),
        pltpu.VMEM((3, 2, R, width), f32),
        pltpu.SemaphoreType.DMA((13, NC)),
        pltpu.SemaphoreType.DMA((13, NC)),
    ]
    vmem = pl.BlockSpec(memory_space=pltpu.VMEM)
    return pl.pallas_call(
        kernel,
        out_shape=jax.ShapeDtypeStruct((NC * R // 4, width), bf),
        in_specs=[pl.BlockSpec(memory_space=pl.ANY)] * 4
        + [vmem] + [pl.BlockSpec(memory_space=pltpu.SMEM)] * 2,
        out_specs=vmem,
        scratch_shapes=scratch,
        compiler_params=pltpu.CompilerParams(
            collective_id=0, has_side_effects=True, vmem_limit_bytes=60 * 2**20
        ),
    )(queries, keys_cache, values_cache, out_weight, early, query_owner, query_offset)


def solution(mesh):
    placed = (P("ctx", "head"), P("ctx", "head"), P("ctx", "head"), P(), P(), P(), P("head", "ctx"))
    return jax.shard_map(
        per_device, mesh=mesh, in_specs=placed, out_specs=P("head", "ctx"), check_vma=False
    )
```

```python
import functools
import math

import jax
import jax.numpy as jnp
from jax import lax
from jax.experimental import pallas as pl
from jax.experimental.pallas import tpu as pltpu
from jax.sharding import PartitionSpec as P

DH = 128
QC = 512
NCH = 2
R = 128
NC = NCH * QC // R
G = 8
MT = 512
HIDE = -1e30
SCALE = math.log2(math.e) / math.sqrt(DH)
MESH = pl.DeviceIdType.MESH
LEAD = 5
TRAIL = 5

S0, S1, S2, G1, G2, G3, O0, O1, O2, H1, H2, H3, Y = range(13)


def kernel(
    queries, keys, values, weight, docs, owner_ref, offset_ref, out_ref,
    q_all, k_ref, v_ref, w_ref, early_ref, load, q_send, q_mine,
    kx, vx, qx, s_buf, p_buf,
    u_buf, r1, t_buf, r2, x2, q_full,
    o_send, o_recv, o_own, o_mix, o_two, o1_send, r1o, o2_send, r2o, x2_send, x2o, w_col, a_full, a_cat,
    y_send, y_recv, send, recv,
):
    shard = k_ref.shape[0]
    loads = [
        pltpu.make_async_copy(queries, q_all, load.at[0]),
        pltpu.make_async_copy(keys, k_ref, load.at[1]),
        pltpu.make_async_copy(values, v_ref, load.at[2]),
        pltpu.make_async_copy(weight, w_ref, load.at[3]),
        pltpu.make_async_copy(docs.at[pl.ds(0, shard // DH)], early_ref, load.at[4]),
    ]
    for one in loads:
        one.start()
    me = lax.axis_index("ctx")
    hd = lax.axis_index("head")
    core = lax.rem(me, 2)
    z = lax.rem(me // 2, 4)
    x = me // 8
    mine, theirs = core * G, (1 - core) * G

    def at_x(d):
        return {"ctx": (lax.rem(x + d, 4) * 4 + z) * 2 + core}

    def at_z(d):
        return {"ctx": (x * 4 + lax.rem(z + d, 4)) * 2 + core}

    partner = {"ctx": me + 1 - 2 * core}

    def at_y(d):
        return {"head": lax.rem(hd + d, 4)}

    barrier = pltpu.get_barrier_semaphore()
    for d in (1, 2, 3):
        for dev in (at_x(d), at_z(d), at_y(d)):
            pl.semaphore_signal(barrier, inc=1, device_id=dev, device_id_type=MESH)
    pl.semaphore_signal(barrier, inc=1, device_id=partner, device_id_type=MESH)

    eye = lax.broadcasted_iota(jnp.int32, (R, R), 0) == lax.broadcasted_iota(jnp.int32, (R, R), 1)

    def prepare():
        for one in loads[1:]:
            one.wait()
        for j in range(2):
            kx[j, 0:DH, :] = k_ref[:, j * DH : (j + 1) * DH].T
            vx[j, :, 0:DH] = v_ref[:, j * DH : (j + 1) * DH]
            vx[j, :, DH : 2 * DH] = jnp.ones((shard, DH), jnp.bfloat16)
        for g in range(G):
            qx[g * R : (g + 1) * R, DH : 2 * DH] = jnp.where(eye, 1.0, 0.0).astype(jnp.bfloat16)


    def put(src, dst, step, c, dev):
        pltpu.make_async_remote_copy(
            src_ref=src, dst_ref=dst, send_sem=send.at[step, c], recv_sem=recv.at[step, c],
            device_id=dev, device_id_type=MESH,
        ).start()

    def get(like, step, c):
        pltpu.make_async_copy(like, like, send.at[step, c]).wait()
        pltpu.make_async_copy(like, like, recv.at[step, c]).wait()

    def quarter(i):
        return pl.ds(pl.multiple_of(i * 32, 32), 32)

    def pick_rows(c):
        which = c // (NC // NCH)
        row = lax.broadcasted_iota(jnp.int32, (R, shard), 0) + (offset_ref[which] + lax.rem(c, NC // NCH) * R)
        here = (jnp.zeros((R, shard), jnp.int32) + owner_ref[which]) == me
        hit = (row == lax.broadcasted_iota(jnp.int32, (R, shard), 1)) & here
        pick = jnp.where(hit, 1.0, 0.0).astype(jnp.bfloat16)
        got = jnp.dot(pick, q_all[...], preferred_element_type=jnp.float32).astype(jnp.bfloat16)
        for g in range(G):
            low, high = got[:, g * DH : (g + 1) * DH], got[:, (G + g) * DH : (G + g + 1) * DH]
            q_mine[lax.rem(c, 2), g] = jnp.where(core == 0, low, high)
            q_send[lax.rem(c, 2), g] = jnp.where(core == 0, high, low)

    def q0_start(c):
        pick_rows(c)
        put(q_send.at[lax.rem(c, 2)], u_buf.at[c], S0, c, partner)

    def q1_start(c):
        get(u_buf.at[c], S0, c)
        for g in range(G):
            u_buf[c, g] = u_buf[c, g] + q_mine[lax.rem(c, 2), g]
        for d in (1, 2, 3):
            put(u_buf.at[c, lax.rem(x + d, 4)], r1.at[c, d - 1], S1, c, at_x(d))
            put(u_buf.at[c, 4 + lax.rem(z + d, 4)], r1.at[c, 2 + d], S1, c, at_z(d))

    def sum1(c):
        get(r1.at[c], S1, c)
        t_buf[c, 0] = (u_buf[c, x] + r1[c, 0]) + (r1[c, 1] + r1[c, 2])
        t_buf[c, 1] = (u_buf[c, 4 + z] + r1[c, 3]) + (r1[c, 4] + r1[c, 5])

    def q2_start(c):
        sum1(c)
        for d in (1, 2, 3):
            put(t_buf.at[c, 0, quarter(lax.rem(z + d, 4))], r2.at[c, d - 1], S2, c, at_z(d))
            put(t_buf.at[c, 1, quarter(lax.rem(x + d, 4))], r2.at[c, 2 + d], S2, c, at_x(d))

    def q2_first(c):
        sum1(c)
        for d in (1, 2, 3):
            put(t_buf.at[c, 0], x2.at[d - 1], S2, c, at_z(d))
            put(t_buf.at[c, 1], x2.at[2 + d], S2, c, at_x(d))

    def gather1(full, c, step):
        a = full.at[c, mine + x, quarter(z)]
        b = full.at[c, mine + 4 + z, quarter(x)]
        for d in (1, 2, 3):
            put(a, a, step, c, at_z(d))
            put(b, b, step, c, at_x(d))

    def gather2(full, c, step):
        a, b = full.at[c, mine + x], full.at[c, mine + 4 + z]
        for d in (1, 2, 3):
            put(a, a, step, c, at_x(d))
            put(b, b, step, c, at_z(d))

    def gather3(full, c, step):
        get(r1.at[c], step - 1, c)
        half = full.at[c, pl.ds(mine, G)]
        put(half, half, step, c, partner)

    def q3_start(c):
        get(r2.at[c], S2, c)
        q_full[c, mine + x, quarter(z), :] = (t_buf[c, 0, quarter(z), :] + r2[c, 0]) + (r2[c, 1] + r2[c, 2])
        q_full[c, mine + 4 + z, quarter(x), :] = (t_buf[c, 1, quarter(x), :] + r2[c, 3]) + (r2[c, 4] + r2[c, 5])
        gather1(q_full, c, G1)

    def q3_first(c):
        get(x2, S2, c)
        q_full[c, mine + x] = (t_buf[c, 0] + x2[0]) + (x2[1] + x2[2])
        q_full[c, mine + 4 + z] = (t_buf[c, 1] + x2[3]) + (x2[4] + x2[5])
        gather2(q_full, c, G2)

    def q4_start(c):
        get(r2.at[c], G1, c)
        gather2(q_full, c, G2)

    def hide(c):
        which = c // (NC // NCH)
        begin = owner_ref[which] * shard + offset_ref[which] + lax.rem(c, NC // NCH) * R
        pos = (lax.broadcasted_iota(jnp.int32, (R, R), 0) + begin).astype(jnp.float32)
        lo = jnp.zeros((R, R), jnp.float32)
        early = early_ref[...]
        for d in range(1, 4):
            bound = jnp.sum(jnp.where(early < d, 1.0, 0.0), axis=0, keepdims=True)
            bound = jnp.broadcast_to(jnp.sum(bound, axis=1, keepdims=True), (R, R))
            lo = jnp.where((bound <= pos) & (bound < float(shard)), jnp.maximum(lo, bound), lo)
        here = (jnp.zeros((R, R), jnp.int32) + me * shard).astype(jnp.float32)
        lo, hi = lo - here, pos - here
        lane = lax.broadcasted_iota(jnp.int32, (R, R), 1).astype(jnp.float32)
        for i in range(shard // R):
            pos = lane + float(i * R)
            bias = jnp.where((pos >= lo) & (pos <= hi), 0.0, HIDE).astype(jnp.bfloat16)
            for j in range(2):
                kx[j, DH : 2 * DH, i * R : (i + 1) * R] = bias

    def attend(c, j, dest):
        first = j * G
        for g in range(G):
            qx[g * R : (g + 1) * R, 0:DH] = q_full[c, first + g]
        tiles = G * R // MT

        def score(t):
            s_buf[t] = jnp.dot(qx[t * MT : (t + 1) * MT, :], kx[j], preferred_element_type=jnp.float32)

        score(0)
        for t in range(tiles):
            if t + 1 < tiles:
                score(t + 1)
            s = s_buf[t]
            top = jnp.max(s, axis=1, keepdims=True) * SCALE
            p_buf[t] = jnp.exp2(s * SCALE - top).astype(jnp.bfloat16)
            o = jnp.dot(p_buf[t], vx[j], preferred_element_type=jnp.float32)
            total = o[:, DH : 2 * DH]
            mean = o[:, 0:DH] / total
            lse = top + jnp.log2(total)
            for i in range(MT // R):
                g = t * (MT // R) + i
                dest[g, 0:R, :] = mean[i * R : (i + 1) * R]
                flat = jnp.sum(jnp.where(eye, lse[i * R : (i + 1) * R], 0.0), axis=0, keepdims=True)
                dest[g, R : R + 8, :] = jnp.broadcast_to(flat, (8, R))

    def column(v):
        return jnp.broadcast_to(v, (R, R)).T

    def merge_stats(parts):
        top = functools.reduce(jnp.maximum, parts)
        ws = [jnp.exp2(p - top) for p in parts]
        total = functools.reduce(jnp.add, ws)
        return [w / total for w in ws], top + jnp.log2(total)

    def pieces3(v):
        a = v.astype(jnp.bfloat16)
        rest = v - a.astype(jnp.float32)
        b = rest.astype(jnp.bfloat16)
        c = (rest - b.astype(jnp.float32)).astype(jnp.bfloat16)
        row = lax.broadcasted_iota(jnp.int32, (16, R), 0)
        full = [jnp.broadcast_to(p.astype(jnp.float32), (16, R)) for p in (a, b, c)]
        return jnp.where(row == 0, full[0], jnp.where(row == 1, full[1], jnp.where(row == 2, full[2], 0.0))).astype(jnp.bfloat16)

    def whole3(block):
        f = block.astype(jnp.float32)
        return (f[0:1] + f[1:2]) + f[2:3]

    def merge1(c, side):
        for g in range(G):
            (wa, _), lse = merge_stats([o_own[g, R : R + 1, :], o_recv[c, g, R : R + 1, :]])
            wa = column(wa)
            mixed = o_own[g, 0:R, :] * wa + o_recv[c, g, 0:R, :] * (1.0 - wa)
            o_mix[side, g, 0:R, :] = mixed
            o_mix[side, g, R : R + 8, :] = jnp.broadcast_to(lse, (8, R))
            o1_send[side, g, 0:R, :] = mixed.astype(jnp.bfloat16)
            o1_send[side, g, R : R + 16, :] = pieces3(lse)

    def send1(c):
        for d in (1, 2, 3):
            put(o1_send.at[lax.rem(c, 2), lax.rem(x + d, 4)], r1o.at[c, d - 1], O1, c, at_x(d))
            put(o1_send.at[lax.rem(c, 2), 4 + lax.rem(z + d, 4)], r1o.at[c, 2 + d], O1, c, at_z(d))

    def merge_four(own, others):
        stats = [own[R : R + 1, :]] + [whole3(o[R : R + 16, :]) for o in others]
        ws, lse = merge_stats(stats)
        mixed = own[0:R, :] * column(ws[0])
        for o, w in zip(others, ws[1:]):
            mixed += o[0:R, :].astype(jnp.float32) * column(w)
        return mixed, lse

    def merge2(c, side):
        for i, at in ((0, x), (1, 4 + z)):
            mixed, lse = merge_four(o_mix[side, at], [r1o[c, 3 * i + d] for d in range(3)])
            o_two[side, i, 0:R, :] = mixed
            o_two[side, i, R : R + 8, :] = jnp.broadcast_to(lse, (8, R))
            coded = pieces3(lse)
            for q in range(4):
                o2_send[side, i, q, 0:32, :] = mixed[q * 32 : (q + 1) * 32].astype(jnp.bfloat16)
                o2_send[side, i, q, 32:48, :] = coded

    def send2(c):
        for d in (1, 2, 3):
            zd, xd = lax.rem(z + d, 4), lax.rem(x + d, 4)
            put(o2_send.at[lax.rem(c, 2), 0, zd], r2o.at[c, d - 1], O2, c, at_z(d))
            put(o2_send.at[lax.rem(c, 2), 1, xd], r2o.at[c, 2 + d], O2, c, at_x(d))

    def merge3(c, side):
        for i, at, part in ((0, x, z), (1, 4 + z, x)):
            stats = [o_two[side, i, R : R + 1, :]] + [whole3(r2o[c, 3 * i + d, 32:48, :]) for d in range(3)]
            ws, _ = merge_stats(stats)
            for d in range(4):
                w_col[i, d] = column(ws[d])
            mixed = o_two[side, i, quarter(part), :] * w_col[i, 0, quarter(part), :]
            for d in range(3):
                mixed += r2o[c, 3 * i + d, 0:32, :].astype(jnp.float32) * w_col[i, 1 + d, quarter(part), :]
            a_full[c, mine + at, quarter(part), :] = mixed.astype(jnp.bfloat16)

    def merge2_last(c, side):
        for i, at in ((0, x), (1, 4 + z)):
            mixed, lse = merge_four(o_mix[side, at], [r1o[c, 3 * i + d] for d in range(3)])
            o_two[side, i, 0:R, :] = mixed
            o_two[side, i, R : R + 8, :] = jnp.broadcast_to(lse, (8, R))
            x2_send[i, 0:R, :] = mixed.astype(jnp.bfloat16)
            x2_send[i, R : R + 16, :] = pieces3(lse)
        for d in (1, 2, 3):
            put(x2_send.at[0], x2o.at[d - 1], O2, c, at_z(d))
            put(x2_send.at[1], x2o.at[2 + d], O2, c, at_x(d))

    def merge3_last(c, side):
        get(x2o, O2, c)
        for i, at in ((0, x), (1, 4 + z)):
            mixed, _ = merge_four(o_two[side, i], [x2o[3 * i + d] for d in range(3)])
            a_full[c, mine + at] = mixed.astype(jnp.bfloat16)
        gather2(a_full, c, H2)

    def project(c):
        get(a_full.at[c, pl.ds(0, G)], H3, c)
        for h in range(2 * G):
            a_cat[:, h * DH : (h + 1) * DH] = a_full[c, h]
        y_send[c] = jnp.dot(a_cat[...], w_ref[...], preferred_element_type=jnp.float32)
        owner = c // 2
        slot = lax.rem(c, 2)
        d = lax.rem(owner - hd + 4, 4)

        @pl.when(d > 0)
        def _():
            put(y_send.at[c], y_recv.at[d - 1, slot], Y, c, at_y(d))

    def when(c, do):
        pl.when((c >= 0) & (c < NC))(functools.partial(do, c))

    def when_in(c, first, last, do):
        pl.when((c >= first) & (c <= last))(functools.partial(do, c))

    def query_steps(t):
        def only(at, do):
            pl.when(t == at)(functools.partial(do, 0))

        only(-2, q3_first)
        only(-3, q2_first)
        only(-4, q1_start)
        when(t + 1, lambda c: gather3(q_full, c, G3))
        when_in(t + 2, 1, NC - 1, q4_start)
        when_in(t + 3, 1, NC - 1, q3_start)
        when_in(t + 4, 1, NC - 1, q2_start)
        when_in(t + 5, 1, NC - 1, q1_start)
        when_in(t + 6, 1, NC - 1, q0_start)

    def before(t, carry):
        query_steps(t)
        pl.when(t == 1 - LEAD)(prepare)
        return carry

    def valid(c):
        return jnp.where(c < 0, NC, c)

    o_own[...] = jnp.zeros_like(o_own)
    o_mix[...] = jnp.zeros_like(o_mix)
    o_two[...] = jnp.zeros_like(o_two)
    o_recv[NC] = jnp.zeros(o_recv.shape[1:], jnp.float32)
    r1o[NC] = jnp.zeros(r1o.shape[1:], jnp.bfloat16)
    r2o[NC] = jnp.zeros(r2o.shape[1:], jnp.bfloat16)

    def h2_start(c):
        get(r2.at[c], H1, c)
        gather2(a_full, c, H2)

    def during(t, carry):
        even, odd = lax.rem(t, 2), lax.rem(t + 1, 2)
        get(u_buf.at[t], G3, t)
        when(t - 1, lambda c: get(o_recv.at[c], O0, c))
        hide(t)
        attend(t, 1 - core, o_send)
        merge1(valid(t - 1), odd)
        put(o_send, o_recv.at[t], O0, t, partner)
        when(t - 1, send1)
        query_steps(t)
        when(t - 6, project)
        when(t - 5, lambda c: gather3(a_full, c, H3))
        when(t - 4, h2_start)
        when(t - 3, lambda c: get(r2o.at[c], O2, c))
        when(t - 2, lambda c: get(r1o.at[c], O1, c))
        attend(t, core, o_own)
        merge3(valid(t - 3), odd)
        merge2(valid(t - 2), even)
        when(t - 2, send2)
        when(t - 3, lambda c: gather1(a_full, c, H1))
        return carry

    def after(t, carry):
        even, odd = lax.rem(t, 2), lax.rem(t + 1, 2)

        def last1(c):
            get(o_recv.at[c], O0, c)
            merge1(c, odd)
            send1(c)

        def last3(c):
            get(r2o.at[c], O2, c)
            merge3(c, odd)
            gather1(a_full, c, H1)

        def last2(c):
            get(r1o.at[c], O1, c)
            merge2(c, even)
            send2(c)

        @pl.when(t == NC + 1)
        def _():
            get(r1o.at[NC - 1], O1, NC - 1)
            merge2_last(NC - 1, (NC - 1) % 2)

        @pl.when(t == NC + 2)
        def _():
            merge3_last(NC - 1, (NC - 1) % 2)

        @pl.when(t == NC + 3)
        def _():
            gather3(a_full, NC - 1, H3)

        when(t - 1, last1)
        when_in(t - 3, 0, NC - 2, last3)
        when_in(t - 2, 0, NC - 2, last2)
        when_in(t - 4, 0, NC - 2, h2_start)
        when_in(t - 5, 0, NC - 2, lambda c: gather3(a_full, c, H3))
        when_in(t - 6, 0, NC - 2, project)

        @pl.when(t == NC + 4)
        def _():
            project(NC - 1)

        return carry

    loads[0].wait()
    pick_rows(0)
    pl.semaphore_wait(barrier, 10)
    put(q_send.at[0], u_buf.at[0], S0, 0, partner)
    lax.fori_loop(-LEAD, 0, before, 0)
    lax.fori_loop(0, NC, during, 0)
    lax.fori_loop(NC, NC + TRAIL, after, 0)

    for c in range(NC):
        d = lax.rem(c // 2 - hd + 4, 4)

        @pl.when(d > 0)
        def _():
            pltpu.make_async_copy(y_send.at[c], y_send.at[c], send.at[Y, c]).wait()

    for i in range(2):
        c = hd * 2 + i
        pltpu.make_async_copy(y_recv.at[:, i], y_recv.at[:, i], recv.at[Y, c]).wait()
        total = (y_send[c] + y_recv[0, i]) + (y_recv[1, i] + y_recv[2, i])
        out_ref[i * R : (i + 1) * R, :] = total.astype(jnp.bfloat16)


def per_device(queries, keys_cache, values_cache, doc_ids, query_owner, query_offset, out_weight):
    shard = keys_cache.shape[0]
    docs = doc_ids.reshape(-1, DH)
    width = out_weight.shape[1]
    bf, f32 = jnp.bfloat16, jnp.float32
    scratch = [
        pltpu.VMEM(queries.shape, bf),
        pltpu.VMEM(keys_cache.shape, bf),
        pltpu.VMEM(values_cache.shape, bf),
        pltpu.VMEM(out_weight.shape, bf),
        pltpu.VMEM((shard // DH, DH), jnp.int32),
        pltpu.SemaphoreType.DMA((5,)),
        pltpu.VMEM((2, G, R, DH), bf),
        pltpu.VMEM((2, G, R, DH), bf),
        pltpu.VMEM((2, 2 * DH, shard), bf),
        pltpu.VMEM((2, shard, 2 * DH), bf),
        pltpu.VMEM((G * R, 2 * DH), bf),
        pltpu.VMEM((2, MT, shard), f32),
        pltpu.VMEM((2, MT, shard), bf),
        pltpu.VMEM((NC, G, R, DH), bf),
        pltpu.VMEM((NC, 6, R, DH), bf),
        pltpu.VMEM((NC, 2, R, DH), bf),
        pltpu.VMEM((NC, 6, 32, DH), bf),
        pltpu.VMEM((6, R, DH), bf),
        pltpu.VMEM((NC, 2 * G, R, DH), bf),
        pltpu.VMEM((G, R + 8, DH), f32),
        pltpu.VMEM((NC + 1, G, R + 8, DH), f32),
        pltpu.VMEM((G, R + 8, DH), f32),
        pltpu.VMEM((2, G, R + 8, DH), f32),
        pltpu.VMEM((2, 2, R + 8, DH), f32),
        pltpu.VMEM((2, G, R + 16, DH), bf),
        pltpu.VMEM((NC + 1, 6, R + 16, DH), bf),
        pltpu.VMEM((2, 2, 4, 48, DH), bf),
        pltpu.VMEM((NC + 1, 6, 48, DH), bf),
        pltpu.VMEM((2, R + 16, DH), bf),
        pltpu.VMEM((6, R + 16, DH), bf),
        pltpu.VMEM((2, 4, R, DH), f32),
        pltpu.VMEM((NC + 1, 2 * G, R, DH), bf),
        pltpu.VMEM((R, 2 * G * DH), bf),
        pltpu.VMEM((NC, R, width), f32),
        pltpu.VMEM((3, 2, R, width), f32),
        pltpu.SemaphoreType.DMA((13, NC)),
        pltpu.SemaphoreType.DMA((13, NC)),
    ]
    vmem = pl.BlockSpec(memory_space=pltpu.VMEM)
    return pl.pallas_call(
        kernel,
        out_shape=jax.ShapeDtypeStruct((NC * R // 4, width), bf),
        in_specs=[pl.BlockSpec(memory_space=pl.ANY)] * 5
        + [pl.BlockSpec(memory_space=pltpu.SMEM)] * 2,
        out_specs=vmem,
        scratch_shapes=scratch,
        compiler_params=pltpu.CompilerParams(
            collective_id=0, has_side_effects=True, vmem_limit_bytes=61 * 2**20
        ),
    )(queries, keys_cache, values_cache, out_weight, docs, query_owner, query_offset)


def solution(mesh):
    placed = (P("ctx", "head"), P("ctx", "head"), P("ctx", "head"), P(), P(), P(), P("head", "ctx"))
    return jax.shard_map(
        per_device, mesh=mesh, in_specs=placed, out_specs=P("head", "ctx"), check_vma=False
    )
```

```python
import functools
import math

import jax
import jax.numpy as jnp
from jax import lax
from jax.experimental import pallas as pl
from jax.experimental.pallas import tpu as pltpu
from jax.sharding import PartitionSpec as P

DH = 128
QC = 512
NCH = 2
R = 128
NC = NCH * QC // R
G = 8
MT = 512
HIDE = -1e30
SCALE = math.log2(math.e) / math.sqrt(DH)
MESH = pl.DeviceIdType.MESH
LEAD = 5
TRAIL = 5

S0, S1, S2, G1, G2, G3, O0, O1, O2, H1, H2, H3, Y = range(13)


def kernel(
    queries, keys, values, weight, docs, owner_ref, offset_ref, out_ref,
    q_all, k_ref, v_ref, w_ref, early_ref, load, q_send, q_mine,
    kx, vx, qx, s_buf, p_buf,
    u_buf, r1, t_buf, r2, x2, q_full,
    o_send, o_recv, o_own, o_mix, o_two, o1_send, r1o, o2_send, r2o, x2_send, x2o, w_col, a_full, a_cat,
    y_send, y_recv, send, recv,
):
    shard = k_ref.shape[0]
    loads = [
        pltpu.make_async_copy(queries, q_all, load.at[0]),
        pltpu.make_async_copy(keys, k_ref, load.at[1]),
        pltpu.make_async_copy(values, v_ref, load.at[2]),
        pltpu.make_async_copy(weight, w_ref, load.at[3]),
        pltpu.make_async_copy(docs.at[pl.ds(0, shard // DH)], early_ref, load.at[4]),
    ]
    for one in loads:
        one.start()
    me = lax.axis_index("ctx")
    hd = lax.axis_index("head")
    core = lax.rem(me, 2)
    z = lax.rem(me // 2, 4)
    x = me // 8
    mine, theirs = core * G, (1 - core) * G

    def at_x(d):
        return {"ctx": (lax.rem(x + d, 4) * 4 + z) * 2 + core}

    def at_z(d):
        return {"ctx": (x * 4 + lax.rem(z + d, 4)) * 2 + core}

    partner = {"ctx": me + 1 - 2 * core}

    def at_y(d):
        return {"head": lax.rem(hd + d, 4)}

    barrier = pltpu.get_barrier_semaphore()
    for d in (1, 2, 3):
        for dev in (at_x(d), at_z(d), at_y(d)):
            pl.semaphore_signal(barrier, inc=1, device_id=dev, device_id_type=MESH)
    pl.semaphore_signal(barrier, inc=1, device_id=partner, device_id_type=MESH)

    eye = lax.broadcasted_iota(jnp.int32, (R, R), 0) == lax.broadcasted_iota(jnp.int32, (R, R), 1)

    def prepare():
        for one in loads[1:]:
            one.wait()
        for j in range(2):
            kx[j, 0:DH, :] = k_ref[:, j * DH : (j + 1) * DH].T
            vx[j, :, 0:DH] = v_ref[:, j * DH : (j + 1) * DH]
            vx[j, :, DH : 2 * DH] = jnp.ones((shard, DH), jnp.bfloat16)
        for g in range(G):
            qx[g * R : (g + 1) * R, DH : 2 * DH] = jnp.where(eye, 1.0, 0.0).astype(jnp.bfloat16)


    def put(src, dst, step, c, dev):
        pltpu.make_async_remote_copy(
            src_ref=src, dst_ref=dst, send_sem=send.at[step, c], recv_sem=recv.at[step, c],
            device_id=dev, device_id_type=MESH,
        ).start()

    def get(like, step, c):
        pltpu.make_async_copy(like, like, recv.at[step, c]).wait()

    def sent(like, step, c):
        pltpu.make_async_copy(like, like, send.at[step, c]).wait()

    def both(like, step, c):
        sent(like, step, c)
        get(like, step, c)

    def quarter(i):
        return pl.ds(pl.multiple_of(i * 32, 32), 32)

    def pick_rows(c):
        which = c // (NC // NCH)
        row = lax.broadcasted_iota(jnp.int32, (R, shard), 0) + (offset_ref[which] + lax.rem(c, NC // NCH) * R)
        here = (jnp.zeros((R, shard), jnp.int32) + owner_ref[which]) == me
        hit = (row == lax.broadcasted_iota(jnp.int32, (R, shard), 1)) & here
        pick = jnp.where(hit, 1.0, 0.0).astype(jnp.bfloat16)
        got = jnp.dot(pick, q_all[...], preferred_element_type=jnp.float32).astype(jnp.bfloat16)
        for g in range(G):
            low, high = got[:, g * DH : (g + 1) * DH], got[:, (G + g) * DH : (G + g + 1) * DH]
            q_mine[lax.rem(c, 2), g] = jnp.where(core == 0, low, high)
            q_send[lax.rem(c, 2), g] = jnp.where(core == 0, high, low)

    def q0_start(c):
        pick_rows(c)
        put(q_send.at[lax.rem(c, 2)], u_buf.at[c], S0, c, partner)

    def q1_start(c):
        both(u_buf.at[c], S0, c)
        for g in range(G):
            u_buf[c, g] = u_buf[c, g] + q_mine[lax.rem(c, 2), g]
        for d in (1, 2, 3):
            put(u_buf.at[c, lax.rem(x + d, 4)], r1.at[c, d - 1], S1, c, at_x(d))
            put(u_buf.at[c, 4 + lax.rem(z + d, 4)], r1.at[c, 2 + d], S1, c, at_z(d))

    def sum1(c):
        get(r1.at[c], S1, c)
        t_buf[c, 0] = (u_buf[c, x] + r1[c, 0]) + (r1[c, 1] + r1[c, 2])
        t_buf[c, 1] = (u_buf[c, 4 + z] + r1[c, 3]) + (r1[c, 4] + r1[c, 5])

    def q2_start(c):
        sum1(c)
        for d in (1, 2, 3):
            put(t_buf.at[c, 0, quarter(lax.rem(z + d, 4))], r2.at[c, d - 1], S2, c, at_z(d))
            put(t_buf.at[c, 1, quarter(lax.rem(x + d, 4))], r2.at[c, 2 + d], S2, c, at_x(d))

    def q2_first(c):
        sum1(c)
        for d in (1, 2, 3):
            put(t_buf.at[c, 0], x2.at[d - 1], S2, c, at_z(d))
            put(t_buf.at[c, 1], x2.at[2 + d], S2, c, at_x(d))

    def gather1(full, c, step):
        a = full.at[c, mine + x, quarter(z)]
        b = full.at[c, mine + 4 + z, quarter(x)]
        for d in (1, 2, 3):
            put(a, a, step, c, at_z(d))
            put(b, b, step, c, at_x(d))

    def gather2(full, c, step):
        a, b = full.at[c, mine + x], full.at[c, mine + 4 + z]
        for d in (1, 2, 3):
            put(a, a, step, c, at_x(d))
            put(b, b, step, c, at_z(d))

    def gather3(full, c, step):
        get(r1.at[c], step - 1, c)
        half = full.at[c, pl.ds(mine, G)]
        put(half, half, step, c, partner)

    def q3_start(c):
        get(r2.at[c], S2, c)
        q_full[c, mine + x, quarter(z), :] = (t_buf[c, 0, quarter(z), :] + r2[c, 0]) + (r2[c, 1] + r2[c, 2])
        q_full[c, mine + 4 + z, quarter(x), :] = (t_buf[c, 1, quarter(x), :] + r2[c, 3]) + (r2[c, 4] + r2[c, 5])
        gather1(q_full, c, G1)

    def q3_first(c):
        get(x2, S2, c)
        q_full[c, mine + x] = (t_buf[c, 0] + x2[0]) + (x2[1] + x2[2])
        q_full[c, mine + 4 + z] = (t_buf[c, 1] + x2[3]) + (x2[4] + x2[5])
        gather2(q_full, c, G2)

    def q4_start(c):
        get(r2.at[c], G1, c)
        gather2(q_full, c, G2)

    def hide(c):
        which = c // (NC // NCH)
        begin = owner_ref[which] * shard + offset_ref[which] + lax.rem(c, NC // NCH) * R
        pos = (lax.broadcasted_iota(jnp.int32, (R, R), 0) + begin).astype(jnp.float32)
        lo = jnp.zeros((R, R), jnp.float32)
        early = early_ref[...]
        for d in range(1, 4):
            bound = jnp.sum(jnp.where(early < d, 1.0, 0.0), axis=0, keepdims=True)
            bound = jnp.broadcast_to(jnp.sum(bound, axis=1, keepdims=True), (R, R))
            lo = jnp.where((bound <= pos) & (bound < float(shard)), jnp.maximum(lo, bound), lo)
        here = (jnp.zeros((R, R), jnp.int32) + me * shard).astype(jnp.float32)
        lo, hi = lo - here, pos - here
        lane = lax.broadcasted_iota(jnp.int32, (R, R), 1).astype(jnp.float32)
        for i in range(shard // R):
            pos = lane + float(i * R)
            bias = jnp.where((pos >= lo) & (pos <= hi), 0.0, HIDE).astype(jnp.bfloat16)
            for j in range(2):
                kx[j, DH : 2 * DH, i * R : (i + 1) * R] = bias

    def attend(c, j, dest):
        first = j * G
        for g in range(G):
            qx[g * R : (g + 1) * R, 0:DH] = q_full[c, first + g]
        tiles = G * R // MT

        def score(t):
            s_buf[t] = jnp.dot(qx[t * MT : (t + 1) * MT, :], kx[j], preferred_element_type=jnp.float32)

        score(0)
        for t in range(tiles):
            if t + 1 < tiles:
                score(t + 1)
            s = s_buf[t]
            top = jnp.max(s, axis=1, keepdims=True) * SCALE
            p_buf[t] = jnp.exp2(s * SCALE - top).astype(jnp.bfloat16)
            o = jnp.dot(p_buf[t], vx[j], preferred_element_type=jnp.float32)
            total = o[:, DH : 2 * DH]
            mean = o[:, 0:DH] / total
            lse = top + jnp.log2(total)
            for i in range(MT // R):
                g = t * (MT // R) + i
                dest[g, 0:R, :] = mean[i * R : (i + 1) * R]
                flat = jnp.sum(jnp.where(eye, lse[i * R : (i + 1) * R], 0.0), axis=0, keepdims=True)
                dest[g, R : R + 8, :] = jnp.broadcast_to(flat, (8, R))

    def column(v):
        return jnp.broadcast_to(v, (R, R)).T

    def merge_stats(parts):
        top = functools.reduce(jnp.maximum, parts)
        ws = [jnp.exp2(p - top) for p in parts]
        total = functools.reduce(jnp.add, ws)
        return [w / total for w in ws], top + jnp.log2(total)

    def pieces3(v):
        a = v.astype(jnp.bfloat16)
        rest = v - a.astype(jnp.float32)
        b = rest.astype(jnp.bfloat16)
        c = (rest - b.astype(jnp.float32)).astype(jnp.bfloat16)
        row = lax.broadcasted_iota(jnp.int32, (16, R), 0)
        full = [jnp.broadcast_to(p.astype(jnp.float32), (16, R)) for p in (a, b, c)]
        return jnp.where(row == 0, full[0], jnp.where(row == 1, full[1], jnp.where(row == 2, full[2], 0.0))).astype(jnp.bfloat16)

    def whole3(block):
        f = block.astype(jnp.float32)
        return (f[0:1] + f[1:2]) + f[2:3]

    def merge1(c, side):
        for g in range(G):
            (wa, _), lse = merge_stats([o_own[g, R : R + 1, :], o_recv[c, g, R : R + 1, :]])
            wa = column(wa)
            mixed = o_own[g, 0:R, :] * wa + o_recv[c, g, 0:R, :] * (1.0 - wa)
            o_mix[side, g, 0:R, :] = mixed
            o_mix[side, g, R : R + 8, :] = jnp.broadcast_to(lse, (8, R))
            o1_send[side, g, 0:R, :] = mixed.astype(jnp.bfloat16)
            o1_send[side, g, R : R + 16, :] = pieces3(lse)

    def send1(c):
        for d in (1, 2, 3):
            put(o1_send.at[lax.rem(c, 2), lax.rem(x + d, 4)], r1o.at[c, d - 1], O1, c, at_x(d))
            put(o1_send.at[lax.rem(c, 2), 4 + lax.rem(z + d, 4)], r1o.at[c, 2 + d], O1, c, at_z(d))

    def merge_four(own, others):
        stats = [own[R : R + 1, :]] + [whole3(o[R : R + 16, :]) for o in others]
        ws, lse = merge_stats(stats)
        mixed = own[0:R, :] * column(ws[0])
        for o, w in zip(others, ws[1:]):
            mixed += o[0:R, :].astype(jnp.float32) * column(w)
        return mixed, lse

    def merge2(c, side):
        for i, at in ((0, x), (1, 4 + z)):
            mixed, lse = merge_four(o_mix[side, at], [r1o[c, 3 * i + d] for d in range(3)])
            o_two[side, i, 0:R, :] = mixed
            o_two[side, i, R : R + 8, :] = jnp.broadcast_to(lse, (8, R))
            coded = pieces3(lse)
            for q in range(4):
                o2_send[side, i, q, 0:32, :] = mixed[q * 32 : (q + 1) * 32].astype(jnp.bfloat16)
                o2_send[side, i, q, 32:48, :] = coded

    def send2(c):
        for d in (1, 2, 3):
            zd, xd = lax.rem(z + d, 4), lax.rem(x + d, 4)
            put(o2_send.at[lax.rem(c, 2), 0, zd], r2o.at[c, d - 1], O2, c, at_z(d))
            put(o2_send.at[lax.rem(c, 2), 1, xd], r2o.at[c, 2 + d], O2, c, at_x(d))

    def merge3(c, side):
        for i, at, part in ((0, x, z), (1, 4 + z, x)):
            stats = [o_two[side, i, R : R + 1, :]] + [whole3(r2o[c, 3 * i + d, 32:48, :]) for d in range(3)]
            ws, _ = merge_stats(stats)
            for d in range(4):
                w_col[i, d] = column(ws[d])
            mixed = o_two[side, i, quarter(part), :] * w_col[i, 0, quarter(part), :]
            for d in range(3):
                mixed += r2o[c, 3 * i + d, 0:32, :].astype(jnp.float32) * w_col[i, 1 + d, quarter(part), :]
            a_full[c, mine + at, quarter(part), :] = mixed.astype(jnp.bfloat16)

    def merge2_last(c, side):
        for i, at in ((0, x), (1, 4 + z)):
            mixed, lse = merge_four(o_mix[side, at], [r1o[c, 3 * i + d] for d in range(3)])
            o_two[side, i, 0:R, :] = mixed
            o_two[side, i, R : R + 8, :] = jnp.broadcast_to(lse, (8, R))
            x2_send[i, 0:R, :] = mixed.astype(jnp.bfloat16)
            x2_send[i, R : R + 16, :] = pieces3(lse)
        for d in (1, 2, 3):
            put(x2_send.at[0], x2o.at[d - 1], O2, c, at_z(d))
            put(x2_send.at[1], x2o.at[2 + d], O2, c, at_x(d))

    def merge3_last(c, side):
        get(x2o, O2, c)
        for i, at in ((0, x), (1, 4 + z)):
            mixed, _ = merge_four(o_two[side, i], [x2o[3 * i + d] for d in range(3)])
            a_full[c, mine + at] = mixed.astype(jnp.bfloat16)
        gather2(a_full, c, H2)

    def project(c):
        get(a_full.at[c, pl.ds(0, G)], H3, c)
        for h in range(2 * G):
            a_cat[:, h * DH : (h + 1) * DH] = a_full[c, h]
        y_send[c] = jnp.dot(a_cat[...], w_ref[...], preferred_element_type=jnp.float32)
        owner = c // 2
        slot = lax.rem(c, 2)
        d = lax.rem(owner - hd + 4, 4)

        @pl.when(d > 0)
        def _():
            put(y_send.at[c], y_recv.at[d - 1, slot], Y, c, at_y(d))

    def when(c, do):
        pl.when((c >= 0) & (c < NC))(functools.partial(do, c))

    def when_in(c, first, last, do):
        pl.when((c >= first) & (c <= last))(functools.partial(do, c))

    def query_steps(t):
        def only(at, do):
            pl.when(t == at)(functools.partial(do, 0))

        only(-2, q3_first)
        only(-3, q2_first)
        only(-4, q1_start)
        when(t + 1, lambda c: gather3(q_full, c, G3))
        when_in(t + 2, 1, NC - 1, q4_start)
        when_in(t + 3, 1, NC - 1, q3_start)
        when_in(t + 4, 1, NC - 1, q2_start)
        when_in(t + 5, 1, NC - 1, q1_start)
        when_in(t + 6, 1, NC - 1, q0_start)

    def before(t, carry):
        query_steps(t)
        pl.when(t == 1 - LEAD)(prepare)
        return carry

    def valid(c):
        return jnp.where(c < 0, NC, c)

    o_own[...] = jnp.zeros_like(o_own)
    o_mix[...] = jnp.zeros_like(o_mix)
    o_two[...] = jnp.zeros_like(o_two)
    o_recv[NC] = jnp.zeros(o_recv.shape[1:], jnp.float32)
    r1o[NC] = jnp.zeros(r1o.shape[1:], jnp.bfloat16)
    r2o[NC] = jnp.zeros(r2o.shape[1:], jnp.bfloat16)

    def h2_start(c):
        get(r2.at[c], H1, c)
        gather2(a_full, c, H2)

    def during(t, carry):
        even, odd = lax.rem(t, 2), lax.rem(t + 1, 2)
        get(u_buf.at[t], G3, t)
        when(t - 1, lambda c: both(o_recv.at[c], O0, c))
        hide(t)
        attend(t, 1 - core, o_send)
        merge1(valid(t - 1), odd)
        put(o_send, o_recv.at[t], O0, t, partner)
        when(t - 1, send1)
        query_steps(t)
        when(t - 6, project)
        when(t - 5, lambda c: gather3(a_full, c, H3))
        when(t - 4, h2_start)
        when(t - 3, lambda c: both(r2o.at[c], O2, c))
        when(t - 2, lambda c: both(r1o.at[c], O1, c))
        attend(t, core, o_own)
        merge3(valid(t - 3), odd)
        merge2(valid(t - 2), even)
        when(t - 2, send2)
        when(t - 3, lambda c: gather1(a_full, c, H1))
        return carry

    def after(t, carry):
        even, odd = lax.rem(t, 2), lax.rem(t + 1, 2)

        def last1(c):
            both(o_recv.at[c], O0, c)
            merge1(c, odd)
            send1(c)

        def last3(c):
            both(r2o.at[c], O2, c)
            merge3(c, odd)
            gather1(a_full, c, H1)

        def last2(c):
            both(r1o.at[c], O1, c)
            merge2(c, even)
            send2(c)

        @pl.when(t == NC + 1)
        def _():
            get(r1o.at[NC - 1], O1, NC - 1)
            merge2_last(NC - 1, (NC - 1) % 2)

        @pl.when(t == NC + 2)
        def _():
            merge3_last(NC - 1, (NC - 1) % 2)

        @pl.when(t == NC + 3)
        def _():
            gather3(a_full, NC - 1, H3)

        when(t - 1, last1)
        when_in(t - 3, 0, NC - 2, last3)
        when_in(t - 2, 0, NC - 2, last2)
        when_in(t - 4, 0, NC - 2, h2_start)
        when_in(t - 5, 0, NC - 2, lambda c: gather3(a_full, c, H3))
        when_in(t - 6, 0, NC - 2, project)

        @pl.when(t == NC + 4)
        def _():
            project(NC - 1)

        return carry

    loads[0].wait()
    pick_rows(0)
    pl.semaphore_wait(barrier, 10)
    put(q_send.at[0], u_buf.at[0], S0, 0, partner)
    lax.fori_loop(-LEAD, 0, before, 0)
    lax.fori_loop(0, NC, during, 0)
    lax.fori_loop(NC, NC + TRAIL, after, 0)

    def drain(c, carry):
        for step in (S1, G2, H2):
            sent(r1.at[c], step, c)
        for step in (G3, H3):
            sent(u_buf.at[c], step, c)

        @pl.when(c > 0)
        def _():
            sent(r2.at[c], S2, c)
            sent(r2.at[c], G1, c)

        @pl.when(c < NC - 1)
        def _():
            sent(r2.at[c], H1, c)

        return carry

    sent(x2, S2, 0)
    sent(r1o.at[NC - 1], O1, NC - 1)
    sent(x2o, O2, NC - 1)
    lax.fori_loop(0, NC, drain, 0)

    for c in range(NC):
        d = lax.rem(c // 2 - hd + 4, 4)

        @pl.when(d > 0)
        def _():
            pltpu.make_async_copy(y_send.at[c], y_send.at[c], send.at[Y, c]).wait()

    for i in range(2):
        c = hd * 2 + i
        pltpu.make_async_copy(y_recv.at[:, i], y_recv.at[:, i], recv.at[Y, c]).wait()
        total = (y_send[c] + y_recv[0, i]) + (y_recv[1, i] + y_recv[2, i])
        out_ref[i * R : (i + 1) * R, :] = total.astype(jnp.bfloat16)


def per_device(queries, keys_cache, values_cache, doc_ids, query_owner, query_offset, out_weight):
    shard = keys_cache.shape[0]
    docs = doc_ids.reshape(-1, DH)
    width = out_weight.shape[1]
    bf, f32 = jnp.bfloat16, jnp.float32
    scratch = [
        pltpu.VMEM(queries.shape, bf),
        pltpu.VMEM(keys_cache.shape, bf),
        pltpu.VMEM(values_cache.shape, bf),
        pltpu.VMEM(out_weight.shape, bf),
        pltpu.VMEM((shard // DH, DH), jnp.int32),
        pltpu.SemaphoreType.DMA((5,)),
        pltpu.VMEM((2, G, R, DH), bf),
        pltpu.VMEM((2, G, R, DH), bf),
        pltpu.VMEM((2, 2 * DH, shard), bf),
        pltpu.VMEM((2, shard, 2 * DH), bf),
        pltpu.VMEM((G * R, 2 * DH), bf),
        pltpu.VMEM((2, MT, shard), f32),
        pltpu.VMEM((2, MT, shard), bf),
        pltpu.VMEM((NC, G, R, DH), bf),
        pltpu.VMEM((NC, 6, R, DH), bf),
        pltpu.VMEM((NC, 2, R, DH), bf),
        pltpu.VMEM((NC, 6, 32, DH), bf),
        pltpu.VMEM((6, R, DH), bf),
        pltpu.VMEM((NC, 2 * G, R, DH), bf),
        pltpu.VMEM((G, R + 8, DH), f32),
        pltpu.VMEM((NC + 1, G, R + 8, DH), f32),
        pltpu.VMEM((G, R + 8, DH), f32),
        pltpu.VMEM((2, G, R + 8, DH), f32),
        pltpu.VMEM((2, 2, R + 8, DH), f32),
        pltpu.VMEM((2, G, R + 16, DH), bf),
        pltpu.VMEM((NC + 1, 6, R + 16, DH), bf),
        pltpu.VMEM((2, 2, 4, 48, DH), bf),
        pltpu.VMEM((NC + 1, 6, 48, DH), bf),
        pltpu.VMEM((2, R + 16, DH), bf),
        pltpu.VMEM((6, R + 16, DH), bf),
        pltpu.VMEM((2, 4, R, DH), f32),
        pltpu.VMEM((NC + 1, 2 * G, R, DH), bf),
        pltpu.VMEM((R, 2 * G * DH), bf),
        pltpu.VMEM((NC, R, width), f32),
        pltpu.VMEM((3, 2, R, width), f32),
        pltpu.SemaphoreType.DMA((13, NC)),
        pltpu.SemaphoreType.DMA((13, NC)),
    ]
    vmem = pl.BlockSpec(memory_space=pltpu.VMEM)
    return pl.pallas_call(
        kernel,
        out_shape=jax.ShapeDtypeStruct((NC * R // 4, width), bf),
        in_specs=[pl.BlockSpec(memory_space=pl.ANY)] * 5
        + [pl.BlockSpec(memory_space=pltpu.SMEM)] * 2,
        out_specs=vmem,
        scratch_shapes=scratch,
        compiler_params=pltpu.CompilerParams(
            collective_id=0, has_side_effects=True, vmem_limit_bytes=61 * 2**20
        ),
    )(queries, keys_cache, values_cache, out_weight, docs, query_owner, query_offset)


def solution(mesh):
    placed = (P("ctx", "head"), P("ctx", "head"), P("ctx", "head"), P(), P(), P(), P("head", "ctx"))
    return jax.shard_map(
        per_device, mesh=mesh, in_specs=placed, out_specs=P("head", "ctx"), check_vma=False
    )
```
